256 devices in a mesh: row: 16 (over y, z_hi), col: 16 (over x, z_lo, core).
Axes of the slice: x: 4, y: 4, z: 8 (z_hi: 4, z_lo: 2; z = z_hi * 2 + z_lo), core: 2. Of those that a mesh axis runs over, the one named last changes fastest.
Arguments:
- matrix: float32 [12288, 12288], P('row', 'col'), as said below
- rotations: float32 [2, 16, 768, 768], P(None, 'row', 'col')
- flips: int32 [2, 16], replicated, may hold values from 0 to 1
Outputs:
- result: float32 [12288, 12288], P('row', 'col')
The draws below stay inside these ranges and needn't reach their ends.
Inputs may be any that keep to these rules, and one draw needn't show every extreme that they name: `matrix`: symmetric.
All inputs are finite; a program needn't handle non-finite values.
Results may differ from the reference program's by a relative error of at most 0.00013.
Values sent between devices are 32-bit elements; how exact they have to be, the bound alone decides.
No kernel may reach another device: no remote copies, remote signals or barrier semaphores. Data moves between devices by JAX's collectives and lax.ppermute only.
A program may use at most 64 MiB of HBM per device.

```python
import jax
import jax.numpy as jnp
from jax import lax

BS = 384
STEPS = 2
PAIRS = 16
N_ROW = 16


def draw_matrix(key, part):
    key = jax.random.fold_in(key, 11)
    order = 2 * BS * N_ROW
    base = jax.random.normal(key, (order, order), jnp.float32)
    return (base + base.T) * 0.7071


def draw_rotations(key, part):
    key = jax.random.fold_in(key, 23)
    wide = 2 * BS
    shape = (STEPS, N_ROW, wide, wide)
    noise = jax.random.normal(key, shape, jnp.float32)
    eye = jnp.eye(wide, dtype=jnp.float32)
    return 0.8 * eye[None, None] + noise * (0.4 / wide ** 0.5)


def touch_ends(values, stream_key, least, high):
    dims = values.shape
    spot = [jax.random.randint(jax.random.fold_in(stream_key, axis), (), 0, dims[axis]) for axis in range(len(dims))]
    values = values.at[tuple(spot)].set(least)
    longest = dims.index(max(dims))
    spot[longest] = (spot[longest] + 1) % dims[longest]
    return values.at[tuple(spot)].set(high)


def setup_inputs(seed: int = 0) -> dict:
    key_of = jax.random.split(jax.random.key(seed), 4)
    matrix = draw_matrix(jax.random.fold_in(key_of[3], 71), 0)
    rotations = draw_rotations(jax.random.fold_in(key_of[3], 71), 0)
    flips = touch_ends(jax.random.randint(key_of[2], (STEPS, PAIRS), 0, 2), jax.random.fold_in(key_of[2], 1), 0, 1).astype(jnp.int32)
    return {"matrix": matrix, "rotations": rotations, "flips": flips}


def round_robin(tops, bots, axis):
    total = tops.shape[axis]
    new_top = jnp.concatenate([lax.slice_in_dim(tops, 0, 1, axis=axis), lax.slice_in_dim(bots, 0, 1, axis=axis), lax.slice_in_dim(tops, 1, total - 1, axis=axis)], axis=axis)
    new_bot = jnp.concatenate([lax.slice_in_dim(bots, 1, total, axis=axis), lax.slice_in_dim(tops, total - 1, total, axis=axis)], axis=axis)
    return new_top, new_bot


def reference(matrix, rotations, flips):
    wide = 2 * BS
    pairs = N_ROW
    order = pairs * wide
    current = matrix
    for step in range(STEPS):
        factor = rotations[step]
        left = jnp.einsum('pwv,pwn->pvn', factor, current.reshape(pairs, wide, order), precision=lax.Precision.HIGHEST, preferred_element_type=jnp.float32)
        left = left.reshape(order, order)
        both = jnp.einsum('npw,pwv->npv', left.reshape(order, pairs, wide), factor, precision=lax.Precision.HIGHEST, preferred_element_type=jnp.float32)
        current = both.reshape(order, order)
        marks = flips[step] == 1
        blocks = current.reshape(pairs, 2, BS, order)
        tops = blocks[:, 0]
        bots = blocks[:, 1]
        select = marks[:, None, None]
        tops, bots = jnp.where(select, bots, tops), jnp.where(select, tops, bots)
        tops, bots = round_robin(tops, bots, 0)
        current = jnp.stack([tops, bots], axis=1).reshape(order, order)
        blocks = current.reshape(order, pairs, 2, BS)
        tops = blocks[:, :, 0]
        bots = blocks[:, :, 1]
        select = marks[None, :, None]
        tops, bots = jnp.where(select, bots, tops), jnp.where(select, tops, bots)
        tops, bots = round_robin(tops, bots, 1)
        current = jnp.stack([tops, bots], axis=2).reshape(order, order)
    return current
```

```python
import functools

import jax
import jax.numpy as jnp
from jax import lax
from jax.experimental import pallas as pl
from jax.experimental.pallas import tpu as pltpu
from jax.sharding import PartitionSpec as P

AXES = ("row", "col")
KERNELS = True
BF = jnp.bfloat16
F32 = jnp.float32


def permute(value, where):
    pairs = []
    for row in range(16):
        for col in range(16):
            y, zh, x, zl, c = where(row // 4, row % 4, col // 4, col // 2 % 2, col % 2)
            target = (4 * (y % 4) + zh % 4) * 16 + 4 * (x % 4) + 2 * (zl % 2) + c % 2
            pairs.append((16 * row + col, target))
    return lax.ppermute(value, AXES, pairs)


def swap_near(i):
    return i ^ 1


def swap_far(i):
    return i if i in (0, 15) else (i + 1 if i % 2 else i - 1)


def move(value, rows, cols):
    return lax.ppermute(
        value,
        AXES,
        [(16 * i + j, 16 * rows(i) + cols(j)) for i in range(16) for j in range(16)],
    )


def gather_row(piece):
    other = permute(piece, lambda y, zh, x, zl, c: (y, zh, x, zl + 1, c))
    both = jnp.concatenate([piece, other], axis=0)
    near = [both] + [
        permute(both, lambda y, zh, x, zl, c, d=d: (y, zh, x - d, zl, c)) for d in (1, 2, 3)
    ]
    far = [permute(v, lambda y, zh, x, zl, c: (y, zh, x, zl, c + 1)) for v in near]
    return near + far


def gather_col(piece):
    half = piece.shape[1] // 2
    turned = permute(piece, lambda y, zh, x, zl, c: (x, zh, y, zl, c))
    four = [
        permute(turned, lambda y, zh, x, zl, c, k=k: (y, (2 * zl + c) ^ k, x, zh >> 1, zh & 1))
        for k in range(4)
    ]
    halves = []
    for h in range(2):
        mine = jnp.concatenate([v[:, h * half : (h + 1) * half] for v in four], axis=0)
        halves.append(
            [mine]
            + [permute(mine, lambda y, zh, x, zl, c, d=d: (y - d, zh, x, zl, c)) for d in (1, 2, 3)]
        )
    return halves


def split(value):
    high = value.astype(BF)
    return high, (value - high.astype(F32)).astype(BF)


def product(ah, al, bh, bl):
    dot = functools.partial(jnp.dot, preferred_element_type=F32)
    return dot(ah, bh) + (dot(ah, bl) + dot(al, bh))


def row_slots(place, shift):
    y, zh, x, zl, c = place
    slots = []
    for dc in range(2):
        for dx in range(4):
            for dl in range(2):
                slots.append((4 * ((x + dx) % 4) + 2 * (zl ^ dl) + (c ^ dc) + shift) % 16)
    return slots


def col_slots(place, shift):
    y, zh, x, zl, c = place
    return [(4 * ((y + dy) % 4) + (zh ^ k) + shift) % 16 for dy in range(4) for k in range(4)]


def call(kernel, outs, args, flops, scratch=()):
    specs = [pl.BlockSpec(memory_space=pltpu.SMEM)]
    specs += [pl.BlockSpec(memory_space=pltpu.VMEM)] * (len(args) - 1)
    nbytes = sum(a.size * a.dtype.itemsize for a in args) + sum(o.size * o.dtype.itemsize for o in outs)
    return pl.pallas_call(
        kernel,
        out_shape=outs,
        in_specs=specs,
        out_specs=[pl.BlockSpec(memory_space=pltpu.VMEM)] * len(outs),
        scratch_shapes=list(scratch),
        compiler_params=pltpu.CompilerParams(vmem_limit_bytes=32 * 2**20),
        cost_estimate=pl.CostEstimate(flops=flops, bytes_accessed=nbytes, transcendentals=0),
    )(*args)


def shape(dims, dtype):
    return jax.ShapeDtypeStruct(dims, dtype)


def assemble(slots, parts, piece):
    flat = jnp.concatenate(parts, axis=0)
    count = flat.shape[0] // piece
    flat = flat.reshape(count, piece, flat.shape[1])
    order = jnp.zeros((count,), jnp.int32).at[slots].set(jnp.arange(count, dtype=jnp.int32))
    return jnp.take(flat, order, axis=0).reshape(count * piece, -1)


def turn_factor(slots, parts, piece):
    wide = parts[0].shape[1]
    if not KERNELS:
        return split(assemble(slots, parts, piece).T)

    def kernel(slots_ref, *refs):
        ins, (high, low, whole) = refs[: len(parts)], refs[len(parts) :]
        per = parts[0].shape[0] // piece
        for n, ref in enumerate(ins):
            for k in range(per):
                at = pl.multiple_of(slots_ref[n * per + k] * piece, 16)
                whole[pl.ds(at, piece), :] = ref[k * piece : (k + 1) * piece, :]
        turned = whole[...].T
        high[...], low[...] = split(turned)

    outs = [shape((wide, wide), BF)] * 2
    return call(kernel, outs, [slots, *parts], 0, [pltpu.VMEM((wide, wide), F32)])


def left(turned, block):
    rows = turned[0].shape[0]
    parts = block if isinstance(block, list) else [block]
    cols = parts[0].shape[1]
    if not KERNELS:
        return split(product(*turned, *split(jnp.concatenate(parts, axis=0))))

    def kernel(_, ah, al, *refs):
        ins, (high, low, xh, xl) = refs[: len(parts)], refs[len(parts) :]
        at = 0
        for ref in ins:
            n = ref.shape[0]
            xh[at : at + n, :], xl[at : at + n, :] = split(ref[...])
            at += n

        @pl.loop(0, rows // 256)
        def _(i):
            here = pl.ds(pl.multiple_of(i * 256, 256), 256)
            out = product(ah[here, :], al[here, :], xh[...], xl[...])
            high[here, :], low[here, :] = split(out)

    outs = [shape((rows, cols), BF)] * 2
    scratch = [pltpu.VMEM((rows, cols), BF)] * 2
    dummy = jnp.zeros((1,), jnp.int32)
    return call(kernel, outs, [dummy, *turned, *parts], 6 * rows * rows * cols, scratch)


def right(slots, lefts, parts, piece):
    rows = lefts[0][0].shape[0]
    wide, cols = rows, parts[0].shape[1]
    half = rows // 2
    if not KERNELS:
        high = jnp.concatenate([v[0] for v in lefts], axis=1)
        low = jnp.concatenate([v[1] for v in lefts], axis=1)
        out = product(high, low, *split(assemble(slots, parts, piece)))
        return out[:half], out[half:]

    def kernel(slots_ref, *refs):
        ls, refs = refs[: 2 * len(lefts)], refs[2 * len(lefts) :]
        ins, (one, two, bh, bl) = refs[: len(parts)], refs[len(parts) :]
        per = parts[0].shape[0] // piece
        for n, ref in enumerate(ins):
            for k in range(per):
                at = pl.multiple_of(slots_ref[n * per + k] * piece, 16)
                h, l = split(ref[k * piece : (k + 1) * piece, :])
                bh[pl.ds(at, piece), :] = h
                bl[pl.ds(at, piece), :] = l
        for out, base in ((one, 0), (two, half)):
            for i in range(0, half, 128):
                total = None
                at = 0
                for n in range(len(lefts)):
                    lh, ll = ls[2 * n], ls[2 * n + 1]
                    k = lh.shape[1]
                    here = slice(base + i, base + i + 128)
                    term = product(lh[here, :], ll[here, :], bh[at : at + k, :], bl[at : at + k, :])
                    total = term if total is None else total + term
                    at += k
                out[i : i + 128, :] = total

    outs = [shape((half, cols), F32)] * 2
    scratch = [pltpu.VMEM((wide, cols), BF)] * 2
    flat = [v for pair in lefts for v in pair]
    return call(kernel, outs, [slots, *flat, *parts], 6 * rows * rows * cols, scratch)


def on_device(matrix, rotations, flips):
    wide = matrix.shape[0]
    half = wide // 2
    piece = rotations.shape[2]
    f = lax.axis_index("row")
    g = lax.axis_index("col")
    place = (f // 4, f % 4, g // 4, g // 2 % 2, g % 2)
    far_first = jnp.where((f % 2 == 1) | (f == 0), 1, 0)

    def own(step):
        mine = rotations[step, 0]
        flip = lax.dynamic_index_in_dim(flips[step], f, keepdims=False)
        ends = jnp.concatenate([mine[:, half:], mine[:, :half]], axis=1)
        return jnp.where((flip ^ far_first) == 1, ends, mine)

    swaps = (swap_near, swap_far)
    first, second = own(0), own(1)
    row1 = gather_row(first)
    col1 = gather_col(first)
    row2 = gather_row(second)
    col2 = gather_col(second)

    def vector(values):
        return jnp.stack([jnp.asarray(v, jnp.int32) for v in values])

    a1 = turn_factor(vector(row_slots(place, 0)), row1, piece)
    t1 = left(a1, matrix)
    slots1 = vector(col_slots(place, 0))
    moved = []
    for h in range(2):
        quads = right(slots1, [t1], col1[h], piece)
        moved.append([move(q, swaps[a], swaps[h]) for a, q in enumerate(quads)])
    shift_f = jnp.where(f % 2 == 0, 8, 0)
    shift_g = jnp.where(g % 2 == 0, 8, 0)
    a2 = turn_factor(vector(row_slots(place, shift_f)), row2, piece)
    t2 = [left(a2, list(moved[h])) for h in range(2)]
    slots2 = vector(col_slots(place, shift_g))
    out = []
    for h in range(2):
        quads = right(slots2, t2, col2[h], piece)
        out.append([move(q, swaps[a], swaps[h]) for a, q in enumerate(quads)])
    even_f, even_g = f % 2 == 0, g % 2 == 0
    tops = [jnp.where(even_f, out[h][1], out[h][0]) for h in range(2)]
    bots = [jnp.where(even_f, out[h][0], out[h][1]) for h in range(2)]
    top = jnp.concatenate(
        [jnp.where(even_g, tops[1], tops[0]), jnp.where(even_g, tops[0], tops[1])], axis=1
    )
    bot = jnp.concatenate(
        [jnp.where(even_g, bots[1], bots[0]), jnp.where(even_g, bots[0], bots[1])], axis=1
    )
    return jnp.concatenate([top, bot], axis=0)


def solution(mesh):
    in_specs = (P("row", "col"), P(None, "row", "col", None), P())
    out_specs = P("row", "col")
    return jax.shard_map(
        on_device, mesh=mesh, in_specs=in_specs, out_specs=out_specs, check_vma=False
    )
```

```python
import functools

import jax
import jax.numpy as jnp
import numpy as np
from jax import lax
from jax.experimental import pallas as pl
from jax.experimental.pallas import tpu as pltpu
from jax.sharding import PartitionSpec as P

AXES = ("row", "col")
KERNELS = True
BF = jnp.bfloat16
F32 = jnp.float32
MIRRORED = (
    0x001A2010015A8412,
    0x92451A411A401A6D,
    0x540354011481D4A1,
    0x198A854AAD8A054C,
    0x4450865A8076A858,
    0x1A4912041A451045,
    0x44211481542194A1,
    0x20CAAC8A2548A580,
    0x084B8056A9498812,
    0x52491A4510451A08,
    0x8081D4A190A1D421,
    0xA5886548A5888504,
    0x0CD2885AA058AC52,
    0x1A4510451841108D,
    0x54B1942504A194A1,
    0x2108A120210A2100,
)
PERMUTATION = (
    0x9C36C97893721B8D878DE1D24B2DB139,
    0xB18D4B398778786C2D39396C1E6CD2E4,
    0x3693D278C6B14E72E42D1E93871BE163,
    0x4BB43927D21E1E2DC9728D2D4E366336,
    0x1ED887E4E44E2D781B72B193931E2772,
    0x396C2DE1782D4E93931B36E44E6CD89C,
    0x634E2D391EB17836279C721BE46CD8C6,
    0xC963D8E19C4B4BC963E4D827C9784B63,
    0x6CB14B6C4B4B72D836636C8D4B3963C9,
    0xC69C1E1E637272272DD2E42D4B3987D8,
    0xB18D1E728DC6E11EC972D2274E27B478,
    0xE163784B63C9D28DD84BC6E42DC94E87,
    0x8D36D2D2391B9CE11E87B19C8DC6D2C6,
    0x36B4B4781B87D89C4ED2D21B87392D1E,
    0x72393678E4E11B1E399CC6722D1E2D39,
    0x9C7887C9D24E9CB1399C1B9C39394BE1,
)


def permute(value, where):
    pairs = []
    for row in range(16):
        for col in range(16):
            y, zh, x, zl, c = where(row // 4, row % 4, col // 4, col // 2 % 2, col % 2)
            target = (4 * (y % 4) + zh % 4) * 16 + 4 * (x % 4) + 2 * (zl % 2) + c % 2
            pairs.append((16 * row + col, target))
    return lax.ppermute(value, AXES, pairs)


def after(value, *others):
    return lax.optimization_barrier((value, *others))[0]


def turn_pieces(piece):
    return permute(piece, lambda y, zh, x, zl, c: (x, 2 * zl + c, y, zh >> 1, zh & 1))


def spread_z(turned):
    return [turned] + [
        permute(turned, lambda y, zh, x, zl, c, k=k: (y, zh ^ k, x, zl, c)) for k in (1, 2, 3)
    ]


def spread_y(mine):
    return [mine] + [
        permute(mine, lambda y, zh, x, zl, c, d=d: (y - d, zh, x, zl, c)) for d in (1, 2, 3)
    ]


def swap(kind, i):
    if kind == 0:
        return i ^ 1
    return i if i in (0, 15) else (i + 1 if i % 2 else i - 1)


@functools.cache
def quadrant_moves():
    edges = [[] for _ in range(256)]
    for p in range(16):
        for q in range(16):
            for a in range(2):
                for b in range(2):
                    source, sent = (swap(a, p), swap(b, q)), 2 * a + b
                    flag = MIRRORED[p] >> (4 * q + sent) & 1
                    if flag:
                        source, sent = source[::-1], 2 * b + a
                    edges[16 * p + q].append((16 * source[0] + source[1], sent, 2 * a + b, flag))
    pairs, table = [[] for _ in range(4)], np.zeros((256, 12), np.int32)
    for device in range(256):
        p, q = divmod(device, 16)
        for source, sent, slot, flag in edges[device]:
            m = PERMUTATION[p] >> (8 * q + 2 * slot) & 3
            pairs[m].append((source, device))
            table[source, m] = sent
            table[device, 4 + m] = slot
            table[device, 8 + m] = flag
    for each in pairs:
        assert len({s for s, _ in each}) == len({d for _, d in each}) == len(each) == 256
    return pairs, table


def move(quads):
    quads = lax.optimization_barrier(quads)
    return [lax.ppermute(q, AXES, pairs) for q, pairs in zip(quads, quadrant_moves()[0])]


def split(value):
    high = value.astype(BF)
    return high, (value - high.astype(F32)).astype(BF)


def product(ah, al, bh, bl):
    dot = functools.partial(jnp.dot, preferred_element_type=F32)
    return dot(ah, bh) + (dot(ah, bl) + dot(al, bh))


def col_slots(y, zh, shift):
    return [(4 * ((y + dy) % 4) + (zh ^ k) + shift) % 16 for dy in range(4) for k in range(4)]


def call(kernel, outs, args, flops, scratch=()):
    specs = [pl.BlockSpec(memory_space=pltpu.SMEM)]
    specs += [pl.BlockSpec(memory_space=pltpu.VMEM)] * (len(args) - 1)
    nbytes = sum(a.size * a.dtype.itemsize for a in args) + sum(o.size * o.dtype.itemsize for o in outs)
    return pl.pallas_call(
        kernel,
        out_shape=outs,
        in_specs=specs,
        out_specs=[pl.BlockSpec(memory_space=pltpu.VMEM)] * len(outs),
        scratch_shapes=list(scratch),
        compiler_params=pltpu.CompilerParams(vmem_limit_bytes=32 * 2**20),
        cost_estimate=pl.CostEstimate(flops=flops, bytes_accessed=nbytes, transcendentals=0),
    )(*args)


def shape(dims, dtype):
    return jax.ShapeDtypeStruct(dims, dtype)


def turn_factor(shift, factor):
    wide = factor.shape[1]
    half = wide // 2
    if not KERNELS:
        return split(jnp.roll(factor, shift[0] * half, axis=0).T)

    def kernel(shift_ref, factor_ref, high, low, whole):
        at = pl.multiple_of(shift_ref[0] * half, half)
        whole[pl.ds(at, half), :] = factor_ref[:half, :]
        whole[pl.ds(half - at, half), :] = factor_ref[half:, :]
        high[...], low[...] = split(whole[...].T)

    outs = [shape((wide, wide), BF)] * 2
    return call(kernel, outs, [shift, factor], 0, [pltpu.VMEM((wide, wide), F32)])


def fill_factor(slots_ref, at, refs, piece, high, low):
    count = refs[0].shape[0] // piece
    for n, ref in enumerate(refs):
        for k in range(count):
            to = pl.ds(pl.multiple_of(slots_ref[at + n * count + k] * piece, 16), piece)
            high[to, :], low[to, :] = split(ref[k * piece : (k + 1) * piece, :])


def plain_factor(slots, parts, piece):
    flat = jnp.concatenate(parts, axis=0)
    count = flat.shape[0] // piece
    flat = flat.reshape(count, piece, flat.shape[1])
    order = jnp.zeros((count,), jnp.int32).at[slots].set(jnp.arange(count, dtype=jnp.int32))
    return split(jnp.take(flat, order, axis=0).reshape(count * piece, -1))


def column_factor(slots, parts, piece):
    wide = parts[0].shape[1]
    if not KERNELS:
        return plain_factor(slots, parts, piece)

    def kernel(slots_ref, *refs):
        ins, (high, low) = refs[: len(parts)], refs[len(parts) :]
        fill_factor(slots_ref, 0, ins, piece, high, low)

    return call(kernel, [shape((wide, wide), BF)] * 2, [slots, *parts], 0)


def left(turned, block):
    wide = block.shape[0]
    if not KERNELS:
        return split(product(*turned, *split(block)))

    def kernel(_, ah, al, ref, high, low, xh, xl):
        xh[...], xl[...] = split(ref[...])

        @pl.loop(0, wide // 256)
        def _(i):
            here = pl.ds(pl.multiple_of(i * 256, 256), 256)
            high[here, :], low[here, :] = split(product(ah[here, :], al[here, :], xh[...], xl[...]))

    outs = [shape((wide, wide), BF)] * 2
    scratch = [pltpu.VMEM((wide, wide), BF)] * 2
    dummy = jnp.zeros((1,), jnp.int32)
    return call(kernel, outs, [dummy, *turned, block], 6 * wide**3, scratch)


def write_quads(info_ref, th, tl, bh, bl, outs):
    half = bh.shape[0] // 2
    for m, out in enumerate(outs):
        sent = info_ref[m]
        rows = pl.ds(pl.multiple_of(((sent >> 1) ^ info_ref[12]) * half, half), half)
        cols = pl.ds(pl.multiple_of(((sent & 1) ^ info_ref[13]) * half, half), half)
        out[...] = product(th[rows, :], tl[rows, :], bh[:, cols], bl[:, cols])


def plain_quads(info, whole):
    half = whole.shape[0] // 2
    quads = whole.reshape(2, half, 2, half).transpose(0, 2, 1, 3).reshape(4, half, half)
    return [jnp.take(quads, info[m] ^ (2 * info[12] + info[13]), axis=0) for m in range(4)]


def right(info, lefts, parts, piece):
    wide = lefts[0].shape[0]
    half = wide // 2
    if not KERNELS:
        return plain_quads(info, product(*lefts, *plain_factor(info[14:], parts, piece)))

    def kernel(info_ref, th, tl, *refs):
        ins, outs, (bh, bl) = refs[: len(parts)], refs[len(parts) : -2], refs[-2:]
        fill_factor(info_ref, 14, ins, piece, bh, bl)
        write_quads(info_ref, th, tl, bh, bl, outs)

    outs = [shape((half, half), F32)] * 4
    scratch = [pltpu.VMEM((wide, wide), BF)] * 2
    return call(kernel, outs, [info, *lefts, *parts], 6 * wide**3, scratch)


def place_quads(table_ref, refs, store, swap_rows=0, swap_cols=0):
    half = refs[0].shape[0]
    for m, ref in enumerate(refs):
        slot = table_ref[4 + m]
        rows = pl.ds(pl.multiple_of(((slot >> 1) ^ swap_rows) * half, half), half)
        cols = pl.ds(pl.multiple_of(((slot & 1) ^ swap_cols) * half, half), half)

        @pl.when(table_ref[8 + m] == 0)
        def _():
            store(rows, cols, ref[...])

        @pl.when(table_ref[8 + m] != 0)
        def _():
            store(rows, cols, ref[...].T)


def plain_block(table, quads, swap_rows=0, swap_cols=0):
    half = quads[0].shape[0]
    whole = jnp.zeros((2 * half, 2 * half), F32)
    for m, quad in enumerate(quads):
        slot = table[4 + m]
        at = (((slot >> 1) ^ swap_rows) * half, ((slot & 1) ^ swap_cols) * half)
        whole = lax.dynamic_update_slice(whole, jnp.where(table[8 + m] == 0, quad, quad.T), at)
    return whole


def both_sides(info, turned, factor, quads):
    half = quads[0].shape[0]
    wide = 2 * half
    if not KERNELS:
        middle = split(product(*turned, *split(plain_block(info, quads))))
        return plain_quads(info, product(*middle, *factor))

    def kernel(info_ref, ah, al, bh, bl, *refs):
        ins, outs, (xh, xl, th, tl) = refs[:4], refs[4:8], refs[8:]

        def store(rows, cols, value):
            xh[rows, cols], xl[rows, cols] = split(value)

        place_quads(info_ref, ins, store)

        @pl.loop(0, wide // 256)
        def _(i):
            here = pl.ds(pl.multiple_of(i * 256, 256), 256)
            th[here, :], tl[here, :] = split(product(ah[here, :], al[here, :], xh[...], xl[...]))

        write_quads(info_ref, th, tl, bh, bl, outs)

    outs = [shape((half, half), F32)] * 4
    scratch = [pltpu.VMEM((wide, wide), BF)] * 4
    return call(kernel, outs, [info, *turned, *factor, *quads], 12 * wide**3, scratch)


def whole_block(table, quads, odd_rows, odd_cols):
    half = quads[0].shape[0]
    if not KERNELS:
        return plain_block(table, quads, 1 - odd_rows, 1 - odd_cols)

    def kernel(info_ref, *refs):
        ins, out = refs[:4], refs[4]

        def store(rows, cols, value):
            out[rows, cols] = value

        place_quads(info_ref, ins, store, 1 - info_ref[12], 1 - info_ref[13])

    info = jnp.concatenate([table, jnp.stack([odd_rows, odd_cols])])
    return call(kernel, [shape((2 * half, 2 * half), F32)], [info, *quads], 0)[0]


def on_device(matrix, rotations, flips):
    wide = matrix.shape[0]
    half = wide // 2
    piece = rotations.shape[2]
    f = lax.axis_index("row")
    g = lax.axis_index("col")
    y, zh = f // 4, f % 4
    odd_f, odd_g = f % 2, g % 2
    far_first = jnp.where((odd_f == 1) | (f == 0), 1, 0)
    table = lax.dynamic_index_in_dim(jnp.asarray(quadrant_moves()[1]), 16 * f + g, keepdims=False)

    def vector(values):
        return jnp.stack([jnp.asarray(v, jnp.int32) for v in values])

    def halves(step):
        marks = flips[step]
        here = [lax.dynamic_index_in_dim(marks, i, keepdims=False) for i in (f, g)]
        return [here[0] ^ far_first, here[1] ^ jnp.where((odd_g == 1) | (g == 0), 1, 0)]

    rows = [lax.all_gather(rotations[s, 0], "col", axis=0, tiled=True) for s in range(2)]
    four = spread_z(turn_pieces(rotations.reshape(2 * piece, wide)))
    col1 = spread_y(jnp.concatenate([v[:piece] for v in four], axis=0))
    mine2 = jnp.concatenate([v[piece:] for v in four], axis=0)
    middle = left(turn_factor(vector([0]), rows[0]), matrix)
    col2 = spread_y(after(mine2, *col1[1:], middle[0]))
    info1 = jnp.concatenate([table, vector(halves(0) + col_slots(y, zh, 0))])
    moved = move(right(info1, middle, col1, piece))
    turned = turn_factor(vector([1 - odd_f]), after(rows[1], moved[0]))
    slots = vector(col_slots(y, zh, 8 - 8 * odd_g))
    factor = column_factor(slots, col2, piece)
    info2 = jnp.concatenate([table, vector(halves(1))])
    moved = move(both_sides(info2, turned, factor, moved))
    return whole_block(table, moved, odd_f, odd_g)


def solution(mesh):
    in_specs = (P("row", "col"), P(None, "row", "col", None), P())
    out_specs = P("row", "col")
    return jax.shard_map(
        on_device, mesh=mesh, in_specs=in_specs, out_specs=out_specs, check_vma=False
    )
```

```python
import functools

import jax
import jax.numpy as jnp
import numpy as np
from jax import lax
from jax.experimental import pallas as pl
from jax.experimental.pallas import tpu as pltpu
from jax.sharding import PartitionSpec as P

AXES = ("row", "col")
KERNELS = True
BF = jnp.bfloat16
F32 = jnp.float32
MIRRORED = (
    (
        0x2018000204428412,
        0x0A4100801A88126D,
        0x50811080400044A1,
        0x249881088D986748,
        0x0408885A8852E850,
        0x020C12081841100C,
        0x4000440154814021,
        0x2088AC880509B400,
        0x081A88F2A8C28440,
        0x12401C4508414004,
        0xC00144A104218020,
        0x81886708A1888180,
        0x8C52A8C2A4580052,
        0x1A41184100041805,
        0xD0A10421402005A1,
        0x2109A4002000A100,
    ),
    (
        0x2018000204428412,
        0x0A4100801A88126D,
        0x50811080400044A1,
        0x249881088D986748,
        0x0408885A8852E850,
        0x020C12081841100C,
        0x4000440154814021,
        0x2088AC880509B400,
        0x081A88F2A8C28440,
        0x12401C4508414004,
        0xC00144A104218020,
        0x81886708A1888180,
        0x8C52A8C2A4580052,
        0x1A41184100041805,
        0xD0A10421402005A1,
        0x2109A4002000A100,
    ),
)
PERMUTATION = (
    (
        0x63C978874EE46C9339E49C1E1E2DD236,
        0x6C4E1E6C6339396C4E78933627932739,
        0xD86C2DC91B2DB4E16C1B1EB4874B7887,
        0x4BC6871B636CC6B1D2781EE1B1C66C1B,
        0x633636638787D86C2793781E36276CD2,
        0x39632DB4D8B4279C274E637872C94E6C,
        0xD293B44E27B472B41E63B43987D8394E,
        0xC61BE49372722D276C934E788D63B18D,
        0x4B2DE4B4D893B12D4E27D2D21E6C9C36,
        0xD24E9CC62D72E4639C368D4EC94E6CC6,
        0xB18D9C931EC9C96C93C9C64E8D7263C6,
        0x1B3972939C9C87D263C6721BC6728D63,
        0x4E7887D8D86C78361E2736D26C4EC939,
        0xD8D8B139932DD21B2DE14EC6636C1BC9,
        0xD86339B11E4EE44B4BE427C6781B2D6C,
        0x634B63E47863394E4B3993B439C94E93,
    ),
    (
        0x63C978874EE46C9339E49C1E1E2DD236,
        0x6C4E1E6C6339396C4E78933627932739,
        0xD86C2DC91B2DB4E16C1B1EB4874B7887,
        0x4BC6871B636CC6B1D2781EE1B1C66C1B,
        0x633636638787D86C2793781E36276CD2,
        0x39632DB4D8B4279C274E637872C94E6C,
        0xD293B44E27B472B41E63B43987D8394E,
        0xC61BE49372722D276C934E788D63B18D,
        0x4B2DE4B4D893B12D4E27D2D21E6C9C36,
        0xD24E9CC62D72E4639C368D4EC94E6CC6,
        0xB18D9C931EC9C96C93C9C64E8D7263C6,
        0x1B3972939C9C87D263C6721BC6728D63,
        0x4E7887D8D86C78361E2736D26C4EC939,
        0xD8D8B139932DD21B2DE14EC6636C1BC9,
        0xD86339B11E4EE44B4BE427C6781B2D6C,
        0x634B63E47863394E4B3993B439C94E93,
    ),
)


def permute(value, where):
    pairs = []
    for row in range(16):
        for col in range(16):
            y, zh, x, zl, c = where(row // 4, row % 4, col // 4, col // 2 % 2, col % 2)
            target = (4 * (y % 4) + zh % 4) * 16 + 4 * (x % 4) + 2 * (zl % 2) + c % 2
            pairs.append((16 * row + col, target))
    return lax.ppermute(value, AXES, pairs)


def after(value, *others):
    return lax.optimization_barrier((value, *others))[0]


def turn_pieces(piece):
    return permute(piece, lambda y, zh, x, zl, c: (x, 2 * zl + c, y, zh >> 1, zh & 1))


def spread_z(turned):
    return [turned] + [
        permute(turned, lambda y, zh, x, zl, c, k=k: (y, zh ^ k, x, zl, c)) for k in (1, 2, 3)
    ]


def spread_y(mine):
    return [mine] + [
        permute(mine, lambda y, zh, x, zl, c, d=d: (y - d, zh, x, zl, c)) for d in (1, 2, 3)
    ]


def swap(kind, i):
    if kind == 0:
        return i ^ 1
    return i if i in (0, 15) else (i + 1 if i % 2 else i - 1)


@functools.cache
def quadrant_moves(step):
    edges = [[] for _ in range(256)]
    for p in range(16):
        for q in range(16):
            for a in range(2):
                for b in range(2):
                    source, sent = (swap(a, p), swap(b, q)), 2 * a + b
                    flag = MIRRORED[step][p] >> (4 * q + sent) & 1
                    if flag:
                        source, sent = source[::-1], 2 * b + a
                    edges[16 * p + q].append((16 * source[0] + source[1], sent, 2 * a + b, flag))
    pairs, table = [[] for _ in range(4)], np.zeros((256, 12), np.int32)
    for device in range(256):
        p, q = divmod(device, 16)
        for source, sent, slot, flag in edges[device]:
            m = PERMUTATION[step][p] >> (8 * q + 2 * slot) & 3
            pairs[m].append((source, device))
            table[source, m] = sent
            table[device, 4 + m] = slot
            table[device, 8 + m] = flag
    for each in pairs:
        assert len({s for s, _ in each}) == len({d for _, d in each}) == len(each) == 256
    return pairs, table


def move(step, quads):
    quads = lax.optimization_barrier(quads)
    return [lax.ppermute(q, AXES, pairs) for q, pairs in zip(quads, quadrant_moves(step)[0])]


def split(value):
    high = value.astype(BF)
    return high, (value - high.astype(F32)).astype(BF)


def product(ah, al, bh, bl):
    dot = functools.partial(jnp.dot, preferred_element_type=F32)
    return dot(ah, bh) + (dot(ah, bl) + dot(al, bh))


def col_slots(y, zh, shift):
    return [(4 * ((y + dy) % 4) + (zh ^ k) + shift) % 16 for dy in range(4) for k in range(4)]


def call(kernel, outs, args, flops, scratch=()):
    specs = [pl.BlockSpec(memory_space=pltpu.SMEM)]
    specs += [pl.BlockSpec(memory_space=pltpu.VMEM)] * (len(args) - 1)
    nbytes = sum(a.size * a.dtype.itemsize for a in args) + sum(o.size * o.dtype.itemsize for o in outs)
    return pl.pallas_call(
        kernel,
        out_shape=outs,
        in_specs=specs,
        out_specs=[pl.BlockSpec(memory_space=pltpu.VMEM)] * len(outs),
        scratch_shapes=list(scratch),
        compiler_params=pltpu.CompilerParams(vmem_limit_bytes=32 * 2**20),
        cost_estimate=pl.CostEstimate(flops=flops, bytes_accessed=nbytes, transcendentals=0),
    )(*args)


def shape(dims, dtype):
    return jax.ShapeDtypeStruct(dims, dtype)


def row_slots(zl, shift):
    return [
        (4 * x + 2 * (zl ^ other) + c + shift) % 16
        for x in range(4)
        for c in range(2)
        for other in range(2)
    ]


def turn_factor(slots, factor, piece):
    wide = factor.shape[1]
    if not KERNELS:
        order = jnp.zeros((16,), jnp.int32).at[slots].set(jnp.arange(16, dtype=jnp.int32))
        return split(jnp.take(factor.reshape(16, piece, wide), order, axis=0).reshape(wide, wide).T)

    def kernel(slots_ref, factor_ref, high, low, whole):
        for n in range(wide // piece):
            to = pl.ds(pl.multiple_of(slots_ref[n] * piece, 16), piece)
            whole[to, :] = factor_ref[n * piece : (n + 1) * piece, :]
        high[...], low[...] = split(whole[...].T)

    outs = [shape((wide, wide), BF)] * 2
    return call(kernel, outs, [slots, factor], 0, [pltpu.VMEM((wide, wide), F32)])


def fill_factor(slots_ref, at, refs, piece, high, low):
    count = refs[0].shape[0] // piece
    for n, ref in enumerate(refs):
        for k in range(count):
            to = pl.ds(pl.multiple_of(slots_ref[at + n * count + k] * piece, 16), piece)
            high[to, :], low[to, :] = split(ref[k * piece : (k + 1) * piece, :])


def plain_factor(slots, parts, piece):
    flat = jnp.concatenate(parts, axis=0)
    count = flat.shape[0] // piece
    flat = flat.reshape(count, piece, flat.shape[1])
    order = jnp.zeros((count,), jnp.int32).at[slots].set(jnp.arange(count, dtype=jnp.int32))
    return split(jnp.take(flat, order, axis=0).reshape(count * piece, -1))


def column_factor(slots, parts, piece):
    wide = parts[0].shape[1]
    if not KERNELS:
        return plain_factor(slots, parts, piece)

    def kernel(slots_ref, *refs):
        ins, (high, low) = refs[: len(parts)], refs[len(parts) :]
        fill_factor(slots_ref, 0, ins, piece, high, low)

    return call(kernel, [shape((wide, wide), BF)] * 2, [slots, *parts], 0)


def left(turned, block):
    wide = block.shape[0]
    if not KERNELS:
        return split(product(*turned, *split(block)))

    def kernel(_, ah, al, ref, high, low, xh, xl):
        xh[...], xl[...] = split(ref[...])

        @pl.loop(0, wide // 256)
        def _(i):
            here = pl.ds(pl.multiple_of(i * 256, 256), 256)
            high[here, :], low[here, :] = split(product(ah[here, :], al[here, :], xh[...], xl[...]))

    outs = [shape((wide, wide), BF)] * 2
    scratch = [pltpu.VMEM((wide, wide), BF)] * 2
    dummy = jnp.zeros((1,), jnp.int32)
    return call(kernel, outs, [dummy, *turned, block], 6 * wide**3, scratch)


def write_quads(info_ref, th, tl, bh, bl, outs):
    half = bh.shape[0] // 2
    for m, out in enumerate(outs):
        sent = info_ref[m]
        rows = pl.ds(pl.multiple_of(((sent >> 1) ^ info_ref[12]) * half, half), half)
        cols = pl.ds(pl.multiple_of(((sent & 1) ^ info_ref[13]) * half, half), half)
        out[...] = product(th[rows, :], tl[rows, :], bh[:, cols], bl[:, cols])


def plain_quads(info, whole):
    half = whole.shape[0] // 2
    quads = whole.reshape(2, half, 2, half).transpose(0, 2, 1, 3).reshape(4, half, half)
    return [jnp.take(quads, info[m] ^ (2 * info[12] + info[13]), axis=0) for m in range(4)]


def right(info, lefts, parts, piece):
    wide = lefts[0].shape[0]
    half = wide // 2
    if not KERNELS:
        return plain_quads(info, product(*lefts, *plain_factor(info[14:], parts, piece)))

    def kernel(info_ref, th, tl, *refs):
        ins, outs, (bh, bl) = refs[: len(parts)], refs[len(parts) : -2], refs[-2:]
        fill_factor(info_ref, 14, ins, piece, bh, bl)
        write_quads(info_ref, th, tl, bh, bl, outs)

    outs = [shape((half, half), F32)] * 4
    scratch = [pltpu.VMEM((wide, wide), BF)] * 2
    return call(kernel, outs, [info, *lefts, *parts], 6 * wide**3, scratch)


def place_quads(table_ref, refs, store, swap_rows=0, swap_cols=0):
    half = refs[0].shape[0]
    for m, ref in enumerate(refs):
        slot = table_ref[4 + m]
        rows = pl.ds(pl.multiple_of(((slot >> 1) ^ swap_rows) * half, half), half)
        cols = pl.ds(pl.multiple_of(((slot & 1) ^ swap_cols) * half, half), half)

        @pl.when(table_ref[8 + m] == 0)
        def _():
            store(rows, cols, ref[...])

        @pl.when(table_ref[8 + m] != 0)
        def _():
            store(rows, cols, ref[...].T)


def plain_block(table, quads, swap_rows=0, swap_cols=0):
    half = quads[0].shape[0]
    whole = jnp.zeros((2 * half, 2 * half), F32)
    for m, quad in enumerate(quads):
        slot = table[4 + m]
        at = (((slot >> 1) ^ swap_rows) * half, ((slot & 1) ^ swap_cols) * half)
        whole = lax.dynamic_update_slice(whole, jnp.where(table[8 + m] == 0, quad, quad.T), at)
    return whole


def both_sides(info, turned, factor, quads):
    half = quads[0].shape[0]
    wide = 2 * half
    if not KERNELS:
        middle = split(product(*turned, *split(plain_block(info, quads))))
        return plain_quads(info, product(*middle, *factor))

    def kernel(info_ref, ah, al, bh, bl, *refs):
        ins, outs, (xh, xl, th, tl) = refs[:4], refs[4:8], refs[8:]

        def store(rows, cols, value):
            xh[rows, cols], xl[rows, cols] = split(value)

        place_quads(info_ref, ins, store)

        @pl.loop(0, wide // 256)
        def _(i):
            here = pl.ds(pl.multiple_of(i * 256, 256), 256)
            th[here, :], tl[here, :] = split(product(ah[here, :], al[here, :], xh[...], xl[...]))

        write_quads(info_ref, th, tl, bh, bl, outs)

    outs = [shape((half, half), F32)] * 4
    scratch = [pltpu.VMEM((wide, wide), BF)] * 4
    return call(kernel, outs, [info, *turned, *factor, *quads], 12 * wide**3, scratch)


def whole_block(table, quads, odd_rows, odd_cols):
    half = quads[0].shape[0]
    if not KERNELS:
        return plain_block(table, quads, 1 - odd_rows, 1 - odd_cols)

    def kernel(info_ref, *refs):
        ins, out = refs[:4], refs[4]

        def store(rows, cols, value):
            out[rows, cols] = value

        place_quads(info_ref, ins, store, 1 - info_ref[12], 1 - info_ref[13])

    info = jnp.concatenate([table, jnp.stack([odd_rows, odd_cols])])
    return call(kernel, [shape((2 * half, 2 * half), F32)], [info, *quads], 0)[0]


def on_device(matrix, rotations, flips):
    wide = matrix.shape[0]
    half = wide // 2
    piece = rotations.shape[2]
    f = lax.axis_index("row")
    g = lax.axis_index("col")
    y, zh, zl = f // 4, f % 4, g // 2 % 2
    odd_f, odd_g = f % 2, g % 2
    far_first = jnp.where((odd_f == 1) | (f == 0), 1, 0)
    tables = np.concatenate([quadrant_moves(step)[1] for step in range(2)], axis=1)
    table = lax.dynamic_index_in_dim(jnp.asarray(tables), 16 * f + g, keepdims=False)
    table1, table2 = table[:12], table[12:]

    def vector(values):
        return jnp.stack([jnp.asarray(v, jnp.int32) for v in values])

    def halves(step):
        marks = flips[step]
        here = [lax.dynamic_index_in_dim(marks, i, keepdims=False) for i in (f, g)]
        return [here[0] ^ far_first, here[1] ^ jnp.where((odd_g == 1) | (g == 0), 1, 0)]

    pieces = rotations.reshape(2 * piece, wide)
    turned = turn_pieces(pieces)
    other = permute(pieces, lambda y, zh, x, zl, c: (y, zh, x, zl + 1, c))
    other = after(other, turned)
    lines = [[4 * x + 2 * l + c for x in range(4) for c in range(2)] for l in range(2)]
    rows = [
        lax.all_gather(
            jnp.concatenate([v[s * piece : (s + 1) * piece] for v in (pieces, other)], axis=0),
            "col",
            axis=0,
            tiled=True,
            axis_index_groups=lines,
        )
        for s in range(2)
    ]
    col1 = spread_y(jnp.concatenate(spread_z(turned[:piece]), axis=0))
    mine2 = jnp.concatenate(spread_z(turned[piece:]), axis=0)

    middle = left(turn_factor(vector(row_slots(zl, 0)), rows[0], piece), matrix)
    col2 = spread_y(after(mine2, *col1[1:], middle[0]))
    info1 = jnp.concatenate([table1, vector(halves(0) + col_slots(y, zh, 0))])
    moved = move(0, right(info1, middle, col1, piece))
    turned = turn_factor(vector(row_slots(zl, 8 - 8 * odd_f)), after(rows[1], moved[0]), piece)
    slots = vector(col_slots(y, zh, 8 - 8 * odd_g))
    factor = column_factor(slots, col2, piece)
    info2 = jnp.concatenate([table2[:4], table1[4:], vector(halves(1))])
    moved = move(1, both_sides(info2, turned, factor, moved))
    return whole_block(table2, moved, odd_f, odd_g)


def solution(mesh):
    in_specs = (P("row", "col"), P(None, "row", "col", None), P())
    out_specs = P("row", "col")
    return jax.shard_map(
        on_device, mesh=mesh, in_specs=in_specs, out_specs=out_specs, check_vma=False
    )
```

```python
import functools

import jax
import jax.numpy as jnp
import numpy as np
from jax import lax
from jax.experimental import pallas as pl
from jax.experimental.pallas import tpu as pltpu
from jax.sharding import PartitionSpec as P

AXES = ("row", "col")
KERNELS = True
BF = jnp.bfloat16
F32 = jnp.float32
MIRRORED = (
    (
        0x2018000204428412,
        0x0A4100801A88126D,
        0x50811080400044A1,
        0x249881088D986748,
        0x0408885A8852E850,
        0x020C12081841100C,
        0x4000440154814021,
        0x2088AC880509B400,
        0x081A88F2A8C28440,
        0x12401C4508414004,
        0xC00144A104218020,
        0x81886708A1888180,
        0x8C52A8C2A4580052,
        0x1A41184100041805,
        0xD0A10421402005A1,
        0x2109A4002000A100,
    ),
    (
        0x0812A012001A8012,
        0x1A491A401A491B6D,
        0x1C811481540154A1,
        0xA18A850A85082588,
        0x80188C5A8050885A,
        0x1A401A491A45100D,
        0xC021148154A194A1,
        0x2008850805088500,
        0x00588050885AA810,
        0x1A491A4512441244,
        0x540154E1148114A1,
        0xA08A054805400508,
        0x4C52A0D8A0588C93,
        0x1A4D10451A401245,
        0x54A11481442114A9,
        0x2100A5000108A100,
    ),
)
PERMUTATION = (
    (
        0x63C978874EE46C9339E49C1E1E2DD236,
        0x6C4E1E6C6339396C4E78933627932739,
        0xD86C2DC91B2DB4E16C1B1EB4874B7887,
        0x4BC6871B636CC6B1D2781EE1B1C66C1B,
        0x633636638787D86C2793781E36276CD2,
        0x39632DB4D8B4279C274E637872C94E6C,
        0xD293B44E27B472B41E63B43987D8394E,
        0xC61BE49372722D276C934E788D63B18D,
        0x4B2DE4B4D893B12D4E27D2D21E6C9C36,
        0xD24E9CC62D72E4639C368D4EC94E6CC6,
        0xB18D9C931EC9C96C93C9C64E8D7263C6,
        0x1B3972939C9C87D263C6721BC6728D63,
        0x4E7887D8D86C78361E2736D26C4EC939,
        0xD8D8B139932DD21B2DE14EC6636C1BC9,
        0xD86339B11E4EE44B4BE427C6781B2D6C,
        0x634B63E47863394E4B3993B439C94E93,
    ),
    (
        0x72B19C4B36E1721E8D1B78E11B2DE139,
        0x724E272DD878399CB14E1E8DE48DC99C,
        0x938D4BD8B4784EB18DD21E87C6B4E44B,
        0xC99C399CD24E8D782DC9D82DE178B12D,
        0x9C2DE4D24B939393879C78D2932DC96C,
        0x4B6CE463B4728D931E1BC693E18D4EB4,
        0xC66CD84EE48D78939C391B934BB1C69C,
        0xD287E44B8DE1934EB46C784E874E63C9,
        0x87B4C99C786C4EC6786C6CD24B78D227,
        0x3636B1D8728D9C9C1ED2C9D2D827C993,
        0xC99C78B4394B9C8D6C2DE1D26C3687D8,
        0x9C1E36788DB1B18D4E78E1E4788D1B36,
        0x4E721E87C64E8736E44BD86CD8B18D4E,
        0x724E6CC9E46C27C9E193366372C6874B,
        0x4E8D8DD8B12DB41E87C6D29C27E44B93,
        0x1E6CB12DE1392D63E18D4EC9D8D8E46C,
    ),
)


def permute(value, where):
    pairs = []
    for row in range(16):
        for col in range(16):
            y, zh, x, zl, c = where(row // 4, row % 4, col // 4, col // 2 % 2, col % 2)
            target = (4 * (y % 4) + zh % 4) * 16 + 4 * (x % 4) + 2 * (zl % 2) + c % 2
            pairs.append((16 * row + col, target))
    return lax.ppermute(value, AXES, pairs)


def after(value, *others):
    return lax.optimization_barrier((value, *others))[0]


def turn_pieces(piece):
    return permute(piece, lambda y, zh, x, zl, c: (x, 2 * zl + c, y, zh >> 1, zh & 1))


def spread_z(turned):
    return [turned] + [
        permute(turned, lambda y, zh, x, zl, c, k=k: (y, zh ^ k, x, zl, c)) for k in (1, 2, 3)
    ]


def spread_y(mine):
    return [mine] + [
        permute(mine, lambda y, zh, x, zl, c, d=d: (y - d, zh, x, zl, c)) for d in (1, 2, 3)
    ]


def swap(kind, i):
    if kind == 0:
        return i ^ 1
    return i if i in (0, 15) else (i + 1 if i % 2 else i - 1)


@functools.cache
def quadrant_moves(step):
    edges = [[] for _ in range(256)]
    for p in range(16):
        for q in range(16):
            for a in range(2):
                for b in range(2):
                    source, sent = (swap(a, p), swap(b, q)), 2 * a + b
                    flag = MIRRORED[step][p] >> (4 * q + sent) & 1
                    if flag:
                        source, sent = source[::-1], 2 * b + a
                    edges[16 * p + q].append((16 * source[0] + source[1], sent, 2 * a + b, flag))
    pairs, table = [[] for _ in range(4)], np.zeros((256, 12), np.int32)
    for device in range(256):
        p, q = divmod(device, 16)
        for source, sent, slot, flag in edges[device]:
            m = PERMUTATION[step][p] >> (8 * q + 2 * slot) & 3
            pairs[m].append((source, device))
            table[source, m] = sent
            table[device, 4 + m] = slot
            table[device, 8 + m] = flag
    for each in pairs:
        assert len({s for s, _ in each}) == len({d for _, d in each}) == len(each) == 256
    return pairs, table


def move(step, quads):
    quads = lax.optimization_barrier(quads)
    return [lax.ppermute(q, AXES, pairs) for q, pairs in zip(quads, quadrant_moves(step)[0])]


def split(value):
    high = value.astype(BF)
    return high, (value - high.astype(F32)).astype(BF)


def product(ah, al, bh, bl):
    dot = functools.partial(jnp.dot, preferred_element_type=F32)
    return dot(ah, bh) + (dot(ah, bl) + dot(al, bh))


def col_slots(y, zh, shift):
    return [(4 * ((y + dy) % 4) + (zh ^ k) + shift) % 16 for dy in range(4) for k in range(4)]


def call(kernel, outs, args, flops, scratch=()):
    specs = [pl.BlockSpec(memory_space=pltpu.SMEM)]
    specs += [pl.BlockSpec(memory_space=pltpu.VMEM)] * (len(args) - 1)
    nbytes = sum(a.size * a.dtype.itemsize for a in args) + sum(o.size * o.dtype.itemsize for o in outs)
    return pl.pallas_call(
        kernel,
        out_shape=outs,
        in_specs=specs,
        out_specs=[pl.BlockSpec(memory_space=pltpu.VMEM)] * len(outs),
        scratch_shapes=list(scratch),
        compiler_params=pltpu.CompilerParams(vmem_limit_bytes=32 * 2**20),
        cost_estimate=pl.CostEstimate(flops=flops, bytes_accessed=nbytes, transcendentals=0),
    )(*args)


def shape(dims, dtype):
    return jax.ShapeDtypeStruct(dims, dtype)


def row_slots(zl, shift):
    return [
        (4 * x + 2 * (zl ^ other) + c + shift) % 16
        for x in range(4)
        for c in range(2)
        for other in range(2)
    ]


def turn_factor(slots, factor, piece):
    wide = factor.shape[1]
    if not KERNELS:
        order = jnp.zeros((16,), jnp.int32).at[slots].set(jnp.arange(16, dtype=jnp.int32))
        return split(jnp.take(factor.reshape(16, piece, wide), order, axis=0).reshape(wide, wide).T)

    def kernel(slots_ref, factor_ref, high, low, whole):
        for n in range(wide // piece):
            to = pl.ds(pl.multiple_of(slots_ref[n] * piece, 16), piece)
            whole[to, :] = factor_ref[n * piece : (n + 1) * piece, :]
        high[...], low[...] = split(whole[...].T)

    outs = [shape((wide, wide), BF)] * 2
    return call(kernel, outs, [slots, factor], 0, [pltpu.VMEM((wide, wide), F32)])


def fill_factor(slots_ref, at, refs, piece, high, low):
    count = refs[0].shape[0] // piece
    for n, ref in enumerate(refs):
        for k in range(count):
            to = pl.ds(pl.multiple_of(slots_ref[at + n * count + k] * piece, 16), piece)
            high[to, :], low[to, :] = split(ref[k * piece : (k + 1) * piece, :])


def plain_factor(slots, parts, piece):
    flat = jnp.concatenate(parts, axis=0)
    count = flat.shape[0] // piece
    flat = flat.reshape(count, piece, flat.shape[1])
    order = jnp.zeros((count,), jnp.int32).at[slots].set(jnp.arange(count, dtype=jnp.int32))
    return split(jnp.take(flat, order, axis=0).reshape(count * piece, -1))


def column_factor(slots, parts, piece):
    wide = parts[0].shape[1]
    if not KERNELS:
        return plain_factor(slots, parts, piece)

    def kernel(slots_ref, *refs):
        ins, (high, low) = refs[: len(parts)], refs[len(parts) :]
        fill_factor(slots_ref, 0, ins, piece, high, low)

    return call(kernel, [shape((wide, wide), BF)] * 2, [slots, *parts], 0)


def left(turned, block):
    wide = block.shape[0]
    if not KERNELS:
        return split(product(*turned, *split(block)))

    def kernel(_, ah, al, ref, high, low, xh, xl):
        xh[...], xl[...] = split(ref[...])

        @pl.loop(0, wide // 256)
        def _(i):
            here = pl.ds(pl.multiple_of(i * 256, 256), 256)
            high[here, :], low[here, :] = split(product(ah[here, :], al[here, :], xh[...], xl[...]))

    outs = [shape((wide, wide), BF)] * 2
    scratch = [pltpu.VMEM((wide, wide), BF)] * 2
    dummy = jnp.zeros((1,), jnp.int32)
    return call(kernel, outs, [dummy, *turned, block], 6 * wide**3, scratch)


def write_quads(info_ref, th, tl, bh, bl, outs):
    half = bh.shape[0] // 2
    for m, out in enumerate(outs):
        sent = info_ref[m]
        rows = pl.ds(pl.multiple_of(((sent >> 1) ^ info_ref[12]) * half, half), half)
        cols = pl.ds(pl.multiple_of(((sent & 1) ^ info_ref[13]) * half, half), half)
        out[...] = product(th[rows, :], tl[rows, :], bh[:, cols], bl[:, cols])


def plain_quads(info, whole):
    half = whole.shape[0] // 2
    quads = whole.reshape(2, half, 2, half).transpose(0, 2, 1, 3).reshape(4, half, half)
    return [jnp.take(quads, info[m] ^ (2 * info[12] + info[13]), axis=0) for m in range(4)]


def right(info, lefts, parts, piece):
    wide = lefts[0].shape[0]
    half = wide // 2
    if not KERNELS:
        return plain_quads(info, product(*lefts, *plain_factor(info[14:], parts, piece)))

    def kernel(info_ref, th, tl, *refs):
        ins, outs, (bh, bl) = refs[: len(parts)], refs[len(parts) : -2], refs[-2:]
        fill_factor(info_ref, 14, ins, piece, bh, bl)
        write_quads(info_ref, th, tl, bh, bl, outs)

    outs = [shape((half, half), F32)] * 4
    scratch = [pltpu.VMEM((wide, wide), BF)] * 2
    return call(kernel, outs, [info, *lefts, *parts], 6 * wide**3, scratch)


def place_quads(table_ref, refs, store, swap_rows=0, swap_cols=0):
    half = refs[0].shape[0]
    for m, ref in enumerate(refs):
        slot = table_ref[4 + m]
        rows = pl.ds(pl.multiple_of(((slot >> 1) ^ swap_rows) * half, half), half)
        cols = pl.ds(pl.multiple_of(((slot & 1) ^ swap_cols) * half, half), half)

        @pl.when(table_ref[8 + m] == 0)
        def _():
            store(rows, cols, ref[...])

        @pl.when(table_ref[8 + m] != 0)
        def _():
            store(rows, cols, ref[...].T)


def plain_block(table, quads, swap_rows=0, swap_cols=0):
    half = quads[0].shape[0]
    whole = jnp.zeros((2 * half, 2 * half), F32)
    for m, quad in enumerate(quads):
        slot = table[4 + m]
        at = (((slot >> 1) ^ swap_rows) * half, ((slot & 1) ^ swap_cols) * half)
        whole = lax.dynamic_update_slice(whole, jnp.where(table[8 + m] == 0, quad, quad.T), at)
    return whole


def both_sides(info, turned, factor, quads):
    half = quads[0].shape[0]
    wide = 2 * half
    if not KERNELS:
        middle = split(product(*turned, *split(plain_block(info, quads))))
        return plain_quads(info, product(*middle, *factor))

    def kernel(info_ref, ah, al, bh, bl, *refs):
        ins, outs, (xh, xl, th, tl) = refs[:4], refs[4:8], refs[8:]

        def store(rows, cols, value):
            xh[rows, cols], xl[rows, cols] = split(value)

        place_quads(info_ref, ins, store)

        @pl.loop(0, wide // 256)
        def _(i):
            here = pl.ds(pl.multiple_of(i * 256, 256), 256)
            th[here, :], tl[here, :] = split(product(ah[here, :], al[here, :], xh[...], xl[...]))

        write_quads(info_ref, th, tl, bh, bl, outs)

    outs = [shape((half, half), F32)] * 4
    scratch = [pltpu.VMEM((wide, wide), BF)] * 4
    return call(kernel, outs, [info, *turned, *factor, *quads], 12 * wide**3, scratch)


def whole_block(table, quads, odd_rows, odd_cols):
    half = quads[0].shape[0]
    if not KERNELS:
        return plain_block(table, quads, 1 - odd_rows, 1 - odd_cols)

    def kernel(info_ref, *refs):
        ins, out = refs[:4], refs[4]

        def store(rows, cols, value):
            out[rows, cols] = value

        place_quads(info_ref, ins, store, 1 - info_ref[12], 1 - info_ref[13])

    info = jnp.concatenate([table, jnp.stack([odd_rows, odd_cols])])
    return call(kernel, [shape((2 * half, 2 * half), F32)], [info, *quads], 0)[0]


def on_device(matrix, rotations, flips):
    wide = matrix.shape[0]
    half = wide // 2
    piece = rotations.shape[2]
    f = lax.axis_index("row")
    g = lax.axis_index("col")
    y, zh, zl = f // 4, f % 4, g // 2 % 2
    odd_f, odd_g = f % 2, g % 2
    far_first = jnp.where((odd_f == 1) | (f == 0), 1, 0)
    tables = np.concatenate([quadrant_moves(step)[1] for step in range(2)], axis=1)
    table = lax.dynamic_index_in_dim(jnp.asarray(tables), 16 * f + g, keepdims=False)
    table1, table2 = table[:12], table[12:]

    def vector(values):
        return jnp.stack([jnp.asarray(v, jnp.int32) for v in values])

    def halves(step):
        marks = flips[step]
        here = [lax.dynamic_index_in_dim(marks, i, keepdims=False) for i in (f, g)]
        return [here[0] ^ far_first, here[1] ^ jnp.where((odd_g == 1) | (g == 0), 1, 0)]

    pieces = rotations.reshape(2 * piece, wide)
    turned = turn_pieces(pieces)
    other = permute(pieces, lambda y, zh, x, zl, c: (y, zh, x, zl + 1, c))
    other = after(other, turned)
    lines = [[4 * x + 2 * l + c for x in range(4) for c in range(2)] for l in range(2)]
    rows = [
        lax.all_gather(
            jnp.concatenate([v[s * piece : (s + 1) * piece] for v in (pieces, other)], axis=0),
            "col",
            axis=0,
            tiled=True,
            axis_index_groups=lines,
        )
        for s in range(2)
    ]
    col1 = spread_y(jnp.concatenate(spread_z(turned[:piece]), axis=0))
    mine2 = jnp.concatenate(spread_z(turned[piece:]), axis=0)

    middle = left(turn_factor(vector(row_slots(zl, 0)), rows[0], piece), matrix)
    col2 = spread_y(after(mine2, *col1[1:], middle[0]))
    info1 = jnp.concatenate([table1, vector(halves(0) + col_slots(y, zh, 0))])
    moved = move(0, right(info1, middle, col1, piece))
    turned = turn_factor(vector(row_slots(zl, 8 - 8 * odd_f)), after(rows[1], moved[0]), piece)
    slots = vector(col_slots(y, zh, 8 - 8 * odd_g))
    factor = column_factor(slots, col2, piece)
    info2 = jnp.concatenate([table2[:4], table1[4:], vector(halves(1))])
    moved = move(1, both_sides(info2, turned, factor, moved))
    return whole_block(table2, moved, odd_f, odd_g)


def solution(mesh):
    in_specs = (P("row", "col"), P(None, "row", "col", None), P())
    out_specs = P("row", "col")
    return jax.shard_map(
        on_device, mesh=mesh, in_specs=in_specs, out_specs=out_specs, check_vma=False
    )
```
